32 devices in a mesh: basin: 2 (over y), srow: 4 (over z), scol: 4 (over x, core).
Axes of the slice: x: 2, y: 2, z: 4, core: 2. Of those that a mesh axis runs over, the one named last changes fastest.
Arguments:
- top_inv: bfloat16 [4096, 2048], P(('basin', 'srow'), 'scol'), parts along dimension 0, may hold values from -0.125 to 0.125
- off_block: bfloat16 [16, 2048, 1024], P(('basin', 'scol'), 'srow'), parts along dimension 0, may hold values from -0.125 to 0.125
- kid_inv: bfloat16 [16, 1024, 1024], P(('basin', 'scol'), 'srow'), parts along dimension 0, may hold values from -0.1875 to 0.1875
- row_struct: int32 [16, 16], P(('basin', 'scol')), parts along dimension 0, may hold values 0 or 1
- labels: int32 [16, 1024], P(('basin', 'scol')), parts along dimension 0, may hold values from 0 to 31, never falling along the last dimension, each value on 1 to 64 neighbouring positions
Outputs:
- top_cov: float32 [4096, 2048], P(('basin', 'srow'), 'scol'), parts along dimension 0
- cross_cov: float32 [16, 2048, 1024], P(('basin', 'scol'), 'srow'), parts along dimension 0
- node_var: float32 [16, 1024], P(('basin', 'scol')), parts along dimension 0
- basin_var: float32 [64], P('basin'), parts along dimension 0
The draws below stay inside these ranges and needn't reach their ends.
There are 2 independent parts, one for each index of `basin`. The reference program is written for one: setup_inputs(seed, part) draws one part's arguments, and reference() takes and returns one part's arrays. A program takes and returns all parts, laid end to end along the dimension named above; each array names one. Nothing has to cross between parts.
Inputs may be any that keep to these rules, and one draw needn't show every extreme that they name: `row_struct`: 1 where the supernode has nonzero entries in that block of 128 rows of the top separator, else 0. `labels`: along each supernode's 1024 nodes the label never falls; every label covers 1 to 64 consecutive nodes of every supernode, and some label covers exactly that many.
All inputs are finite; a program needn't handle non-finite values.
Results may differ from the reference program's by a relative error of at most 0.004.
Values may be sent and summed in bfloat16 or wider, within the bound.
A program may use at most 64 MiB of HBM per device.

```python
import math
import jax
import jax.numpy as jnp
import numpy as np
from jax import lax

NT = 2048
W2 = 1024
RB = 128
G = 32
KIDS = 8
NBLK = 16


def plant(values, stream_key, least, top_value):
    extent = values.shape
    index_at = [jax.random.randint(jax.random.fold_in(stream_key, axis), (), 0, extent[axis]) for axis in range(len(extent))]
    values = values.at[tuple(index_at)].set(least)
    longest = extent.index(max(extent))
    index_at[longest] = (index_at[longest] + 1) % extent[longest]
    return values.at[tuple(index_at)].set(top_value)


def levels(key, shape, shards, least, largest):
    gain = 1.0
    for axis_at, parts in shards:
        steps = jax.random.uniform(jax.random.fold_in(jax.random.fold_in(key, 6), axis_at), (parts,), jnp.float32, least / len(shards), largest / len(shards))
        gain = gain * jnp.repeat(jnp.exp(steps), shape[axis_at] // parts).reshape((-1,) + (1,) * (len(shape) - 1 - axis_at))
    return gain


def length_profile(count, total, bound, lean):
    loads = [(1 << 20) // math.isqrt(grade ** lean) + 1 for grade in range(2, count + 1)]
    spare, holding = total - bound - (count - 1), [1] * (count - 1)
    while spare > 0:
        movable = [i for i in range(count - 1) if holding[i] < bound]
        pool, budget = sum([loads[i] for i in movable]), spare
        for i in movable:
            addition = min(bound - holding[i], max(1, budget * loads[i] // pool), spare)
            holding[i] = holding[i] + addition
            spare = spare - addition
    return np.array([bound] + holding)


def uneven_parts(own_key, amount, total, bound, slope):
    if amount == 2:
        one = jax.random.randint(own_key, (), max(1, total - bound), min(bound, total - 1) + 1)
        return jnp.stack([one, total - one])
    sizes = jnp.asarray(length_profile(amount, total, bound, slope), jnp.int32)
    couples = (amount - 1) // 2
    source_of, taker = sizes[1:1 + 2 * couples:2], sizes[2:2 + 2 * couples:2]
    margin = jnp.minimum(source_of - 1, bound - taker)
    shifted = jax.random.randint(jax.random.fold_in(own_key, 1), (couples,), 0, 1 << 20) % (margin + 1)
    sizes = sizes.at[1:1 + 2 * couples:2].set(source_of - shifted).at[2:2 + 2 * couples:2].set(taker + shifted)
    return sizes[jax.random.permutation(jax.random.fold_in(own_key, 2), amount)]


def scatter_about(stream_key, shape, scale, limit, split=(), kind=jnp.bfloat16):
    array = scale * jax.random.normal(stream_key, shape, jnp.float32)
    if split:
        array = array * levels(stream_key, shape, split, -0.22, 0.18)
    return jnp.clip(array, -limit, limit).astype(kind)


def setup_inputs(seed: int = 0, part: int = 0) -> dict:
    streams_of = jax.random.split(jax.random.key(seed), 6)
    part_splits = jax.random.split(jax.random.fold_in(streams_of[5], part), 6)
    return {
        "top_inv": scatter_about(part_splits[0], (NT, NT), NT ** -0.5, 0.125, ((0, 4), (1, 4))),
        "off_block": scatter_about(part_splits[1], (KIDS, NT, W2), NT ** -0.5, 0.125, ((0, 4), (1, 4))),
        "kid_inv": scatter_about(part_splits[2], (KIDS, W2, W2), W2 ** -0.5, 0.1875, ((0, 4), (1, 4))),
        "row_struct": plant((jax.random.randint(part_splits[3], (KIDS, NBLK), 0, 4) < 3).astype(jnp.int32), jax.random.fold_in(part_splits[3], 1), 0, 1),
        "labels": jax.vmap(lambda own: jnp.searchsorted(jnp.cumsum(uneven_parts(own, G, W2, 2 * W2 // G, 1)), jnp.arange(W2), side="right"))(jax.random.split(part_splits[4], KIDS)).reshape((KIDS, W2)).astype(jnp.int32),
    }


def reference(top_inv, off_block, kid_inv, row_struct, labels):
    node_index = jnp.arange(NT, dtype=jnp.int32)
    above_diag = node_index[None, :] > node_index[:, None]
    diagonal_one = (node_index[None, :] == node_index[:, None]).astype(top_inv.dtype)
    top_factor = jnp.where(above_diag, top_inv, diagonal_one).astype(jnp.bfloat16)
    top_cov = jnp.dot(top_factor, top_factor.T, preferred_element_type=jnp.float32)
    top_half = top_cov.astype(jnp.bfloat16)
    kid_index = jnp.arange(W2, dtype=jnp.int32)
    below_diag = kid_index[:, None] > kid_index[None, :]
    kid_one = (kid_index[:, None] == kid_index[None, :]).astype(kid_inv.dtype)
    kept_rows = row_struct[:, node_index // RB]

    def one_kid(kid_items):
        off_piece, inverse, kept_now = kid_items
        factor = jnp.where(below_diag, inverse, kid_one).astype(jnp.bfloat16)
        masked = jnp.where(kept_now[:, None] != 0, off_piece, jnp.zeros_like(off_piece))
        product = jnp.dot(masked, factor, preferred_element_type=jnp.float32).astype(jnp.bfloat16)
        cross_cov = -jnp.dot(top_half, product, preferred_element_type=jnp.float32)
        variance = jnp.sum(jnp.square(factor.astype(jnp.float32)), axis=0) - jnp.sum(product.astype(jnp.float32) * cross_cov, axis=0)
        return cross_cov, variance

    cross_cov, node_var = lax.map(one_kid, (off_block, kid_inv, kept_rows))
    onehot = (labels[:, :, None] == jnp.arange(G, dtype=jnp.int32)[None, None, :]).astype(jnp.float32)
    label_sum = jnp.einsum("kw,kwg->g", node_var, onehot)
    counts = jnp.sum(onehot, axis=(0, 1))
    return top_cov, cross_cov, node_var, label_sum / counts
```

```python
import jax
import jax.numpy as jnp
from jax import lax
from jax.experimental import pallas as pl
from jax.experimental.pallas import tpu as pltpu
from jax.sharding import PartitionSpec as P

RB = 128
G = 32


def per_device(top_inv, off_block, kid_inv, row_struct, labels):
    row_rank = lax.axis_index("srow")
    col_rank = lax.axis_index("scol")
    rows_top = top_inv.shape[0]
    cols_top = top_inv.shape[1]
    row_ids = row_rank * rows_top + jnp.arange(rows_top, dtype=jnp.int32)
    col_ids = col_rank * cols_top + jnp.arange(cols_top, dtype=jnp.int32)
    diagonal_one = (col_ids[None, :] == row_ids[:, None]).astype(top_inv.dtype)
    top_factor = jnp.where(col_ids[None, :] > row_ids[:, None], top_inv, diagonal_one)
    top_panel = lax.all_gather(top_factor, "srow", axis=0, tiled=True)
    block_sum = lax.psum_scatter(
        lax.dot_general(
            top_panel, top_factor, (((1,), (1,)), ((), ())), preferred_element_type=jnp.float32
        ),
        "scol",
        scatter_dimension=0,
        tiled=True,
    )
    top_cov = block_sum.T
    top_half = lax.all_gather(top_cov.astype(jnp.bfloat16), "scol", axis=1, tiled=True)
    kid_rows = kid_inv.shape[1]
    width = kid_inv.shape[2]
    kid_row_ids = row_rank * kid_rows + jnp.arange(kid_rows, dtype=jnp.int32)
    kid_col_ids = jnp.arange(width, dtype=jnp.int32)
    kid_one = (kid_row_ids[:, None] == kid_col_ids[None, :]).astype(kid_inv.dtype)
    kid_factor = jnp.where(kid_row_ids[:, None] > kid_col_ids[None, :], kid_inv, kid_one)
    local_rows = off_block.shape[1]
    block_ids = (row_rank * local_rows + jnp.arange(local_rows, dtype=jnp.int32)) // RB
    block_hits = (
        block_ids[:, None] == jnp.arange(row_struct.shape[1], dtype=jnp.int32)[None, :]
    ).astype(jnp.int32)
    kept_rows = jnp.sum(row_struct[:, None, :] * block_hits[None, :, :], axis=2)
    masked = jnp.where(kept_rows[:, :, None] != 0, off_block, jnp.zeros_like(off_block))
    product = jnp.einsum(
        "kac,kcw->kaw",
        masked,
        lax.all_gather(kid_factor, "srow", axis=1, tiled=True),
        preferred_element_type=jnp.float32,
    ).astype(jnp.bfloat16)
    image_sum = jnp.einsum(
        "am,kmw->kaw",
        top_half,
        lax.all_gather(product, "srow", axis=1, tiled=True),
        preferred_element_type=jnp.float32,
    )
    cross_cov = -image_sum
    own_part = jnp.sum(jnp.square(kid_factor.astype(jnp.float32)), axis=1) - jnp.sum(
        product.astype(jnp.float32) * cross_cov, axis=1
    )
    node_var = lax.psum(own_part, "srow")
    onehot = (labels[:, :, None] == jnp.arange(G, dtype=jnp.int32)[None, None, :]).astype(
        jnp.float32
    )
    local_counts = jnp.sum(onehot, axis=(0, 1))
    label_sum, counts = lax.psum((jnp.einsum("kw,kwg->g", node_var, onehot), local_counts), "scol")
    basin_var = label_sum / counts
    return (top_cov, cross_cov, node_var, basin_var)

MESH = pl.DeviceIdType.MESH


def dot(a, b, b_dim):
    return lax.dot_general(a, b, (((1,), (b_dim,)), ((), ())), preferred_element_type=jnp.float32)


def fused(f_ref, off_ref, kid_ref, cov_ref, cross_ref, var_ref,
          fall, offb, kidf, prod, th, acc, cbuf, vsum, vgot,
          f_send, f_recv, off_send, off_recv, kid_send, kid_fwd, kid_recv,
          p_send, p_recv, c_send, c_recv, v_send, v_recv):
    b, z, d = lax.axis_index("basin"), lax.axis_index("srow"), lax.axis_index("scol")
    h = lax.rem(d, 2)
    base = d - h
    sib = d + 1 - 2 * h
    across = lax.rem(d + 2, 4)
    far = lax.rem(sib + 2, 4)
    tb = f_ref.shape[0]
    kr = kid_ref.shape[1]
    hw = kid_ref.shape[2] // 2
    keeper = lax.div(z, 2)
    slot = lax.rem(z, 2)
    home = base + keeper
    is_keeper = h == keeper
    pending = []

    barrier = pltpu.get_barrier_semaphore()
    for s in range(1, 16):
        other = lax.rem(z * 4 + d + s, 16)
        pl.semaphore_signal(
            barrier, inc=1, device_id=(b, lax.div(other, 4), lax.rem(other, 4)), device_id_type=MESH
        )
    pl.semaphore_wait(barrier, 15)

    def send(cond, source, target, ssem, rsem, zz, cc):
        copy = pltpu.make_async_remote_copy(
            src_ref=source, dst_ref=target, send_sem=ssem, recv_sem=rsem,
            device_id=(b, zz, cc), device_id_type=MESH,
        )
        pl.when(cond)(lambda: copy.start())
        pending.append((cond, copy))

    def local(cond, source, target, rsem):
        pl.when(cond)(lambda: pltpu.make_async_copy(source, target, rsem).start())

    def arrived(cond, target, rsem):
        pl.when(cond)(lambda: pltpu.make_async_copy(target, target, rsem).wait())

    def fan(s, r, source):
        have = r <= d
        target, rsem = fall.at[r, d], f_recv.at[r * 4 + d]
        send(have & (r <= z) & (z < 3), source, target, f_send.at[s * 5], rsem, jnp.minimum(z + 1, 3), d)
        send(have & (r >= z) & (z > 0), source, target, f_send.at[s * 5 + 1], rsem, jnp.maximum(z - 1, 0), d)
        send(have, source, target, f_send.at[s * 5 + 2], rsem, z, across)
        send(have, source, target, f_send.at[s * 5 + 3], rsem, z, sib)

    order = (z, z + 1 - 2 * slot, jnp.where(z < 2, 2, 1), jnp.where(z < 2, 3, 0))
    local(z <= d, f_ref, fall.at[z, d], f_recv.at[z * 4 + d])
    fan(0, z, f_ref)

    for part in (1, 0):
        cols = pl.ds(part * hw, hw)
        needed = (z >= 2) if part else (z >= 0)
        for i in range(2):
            kid = 2 * h + i
            n = part * 2 + i
            send(kid != z, off_ref.at[i, :, cols], offb.at[part, pl.ds(pl.multiple_of(slot * tb, tb), tb), :],
                 off_send.at[n], off_recv.at[part * 2 + slot], kid, home)
            local(kid == z, off_ref.at[i, :, cols], offb.at[part, pl.ds(pl.multiple_of(slot * tb, tb), tb), :],
                  off_recv.at[part * 2 + slot])
            send((kid != z) & needed, kid_ref.at[i, :, cols], kidf.at[part, z],
                 kid_send.at[n], kid_recv.at[part * 4 + z], kid, d)
            local((kid == z) & needed, kid_ref.at[i, :, cols], kidf.at[part, z], kid_recv.at[part * 4 + z])

    def pass_on(s):
        r = order[s]
        arrived(r <= across, fall.at[r, across], f_recv.at[r * 4 + across])
        send(r <= across, fall.at[r, across], fall.at[r, across], f_send.at[s * 5 + 4],
             f_recv.at[r * 4 + across], z, sib)

    for s in range(1, 4):
        r = order[s]
        arrived(r <= d, fall.at[r, d], f_recv.at[r * 4 + d])
        fan(s, r, fall.at[r, d])
        pass_on(s - 1)
    pass_on(3)
    arrived(z <= d, fall.at[z, d], f_recv.at[z * 4 + d])
    for s in range(4):
        for c in (sib, far):
            arrived(order[s] <= c, fall.at[order[s], c], f_recv.at[order[s] * 4 + c])

    def outer_block(r, c):
        acc[...] = jnp.zeros_like(acc)

        @pl.loop(jnp.maximum(r, c), 4)
        def _(k):
            acc[...] += dot(fall[r, k], fall[c, k], 1)

    @pl.loop(0, 8)
    def _(n):
        i, j = lax.div(n, 4), lax.rem(n, 4)
        outer_block(2 * h + i, j)
        th[i, j] = acc[...].astype(jnp.bfloat16)

    outer_block(z, d)
    cov_ref[...] = acc[...]

    half = pl.multiple_of(h * 2 * tb, 2 * tb)
    for part in (1, 0):
        cols = pl.ds(part * hw, hw)
        low = 2 if part else 0
        for zp in range(low, 4):
            arrived(z >= 0, kidf.at[part, zp], kid_recv.at[part * 4 + zp])
            send(is_keeper, kidf.at[part, zp], kidf.at[part, zp], kid_fwd.at[part * 4 + zp],
                 kid_recv.at[part * 4 + zp], z, sib)
        for q in range(2):
            arrived(z >= 0, offb.at[part, pl.ds(q * tb, tb), :], off_recv.at[part * 2 + q])

        @pl.loop(0, 2 * tb // 256)
        def _(m):
            rows = pl.ds(pl.multiple_of(m * 256, 256), 256)
            lower = kidf[part, 2:4].reshape(2 * kr, hw)
            total = dot(offb[1, rows, :], lower, 0)
            if part == 0:
                total += dot(offb[0, rows, :], kidf[0, 0:2].reshape(2 * kr, hw), 0)
            prod[part, pl.ds(pl.multiple_of(half + m * 256, 256), 256), :] = total.astype(jnp.bfloat16)

        mine = prod.at[part, pl.ds(half, 2 * tb), :]
        send(z >= 0, mine, mine, p_send.at[part], p_recv.at[part], z, sib)

        vsum[part] = jnp.zeros((8, hw), jnp.float32)

        @pl.when(h == 0)
        def _():
            for zp in range(low, 4):
                square = jnp.square(kidf[part, zp].astype(jnp.float32))
                vsum[part] += jnp.sum(square.reshape(kr // 8, 8, hw), axis=0)

        theirs = prod.at[part, pl.ds(pl.multiple_of((1 - h) * 2 * tb, 2 * tb), 2 * tb), :]
        arrived(z >= 0, theirs, p_recv.at[part])
        for i in range(2):
            for m in range(2):
                rows = pl.ds(m * (tb // 2), tb // 2)
                total = dot(th[i, 0, rows, :], prod[part, 0:tb, :], 0)
                for j in range(1, 4):
                    total += dot(th[i, j, rows, :], prod[part, j * tb:(j + 1) * tb, :], 0)
                own = prod[part, pl.ds(pl.multiple_of(half + i * tb + m * (tb // 2), tb // 2), tb // 2), :]
                vsum[part] += jnp.sum((own.astype(jnp.float32) * total).reshape(tb // 16, 8, hw), axis=0)
                cbuf[part, i, rows, :] = (-total).astype(jnp.bfloat16)
            there = 2 * h + i
            send(there != z, cbuf.at[part, i], cross_ref.at[slot, :, cols], c_send.at[part * 2 + i],
                 c_recv.at[part * 2 + slot], there, home)
            local(there == z, cbuf.at[part, i], cross_ref.at[slot, :, cols], c_recv.at[part * 2 + slot])
        for there in range(4):
            to_self = (there == z) & is_keeper
            place = part * 4 + slot * 2 + h
            send(jnp.logical_not(to_self), vsum.at[part], vgot.at[place], v_send.at[part * 4 + there],
                 v_recv.at[place], there, home)
            local(to_self, vsum.at[part], vgot.at[place], v_recv.at[place])

    for part in (1, 0):
        cols = pl.ds(part * hw, hw)
        for q in range(2):
            for hh in range(2):
                arrived(z >= 0, vgot.at[part * 4 + q * 2 + hh], v_recv.at[part * 4 + q * 2 + hh])
            both = vgot[part * 4 + q * 2] + vgot[part * 4 + q * 2 + 1]
            var_ref[q:q + 1, cols] = jnp.sum(both, axis=0, keepdims=True)
    for part in (1, 0):
        for q in range(2):
            place = cross_ref.at[q, :, pl.ds(part * hw, hw)]
            arrived(z >= 0, place, c_recv.at[part * 2 + q])
    for cond, copy in pending:
        pl.when(cond)(copy.wait_send)


def per_device_fused(top_inv, off_block, kid_inv, row_struct, labels):
    row_rank = lax.axis_index("srow")
    col_rank = lax.axis_index("scol")
    tb = top_inv.shape[0]
    row_ids = row_rank * tb + jnp.arange(tb, dtype=jnp.int32)
    col_ids = col_rank * tb + jnp.arange(tb, dtype=jnp.int32)
    diagonal_one = (col_ids[None, :] == row_ids[:, None]).astype(top_inv.dtype)
    top_factor = jnp.where(col_ids[None, :] > row_ids[:, None], top_inv, diagonal_one)
    kr = kid_inv.shape[1]
    width = kid_inv.shape[2]
    hw = width // 2
    kid_row_ids = row_rank * kr + jnp.arange(kr, dtype=jnp.int32)
    kid_col_ids = jnp.arange(width, dtype=jnp.int32)
    kid_one = (kid_row_ids[:, None] == kid_col_ids[None, :]).astype(kid_inv.dtype)
    kid_factor = jnp.where(kid_row_ids[:, None] > kid_col_ids[None, :], kid_inv, kid_one)
    blocks = tb // RB
    kept = lax.dynamic_slice_in_dim(row_struct, row_rank * blocks, blocks, axis=1)
    kept_rows = jnp.repeat(kept, RB, axis=1)
    masked = jnp.where(kept_rows[:, :, None] != 0, off_block, jnp.zeros_like(off_block))
    bf = jnp.bfloat16
    dma = pltpu.SemaphoreType.DMA
    top_cov, cross_half, node_var = pl.pallas_call(
        fused,
        out_shape=(
            jax.ShapeDtypeStruct((tb, tb), jnp.float32),
            jax.ShapeDtypeStruct((2, tb, width), bf),
            jax.ShapeDtypeStruct((2, width), jnp.float32),
        ),
        in_specs=[pl.BlockSpec(memory_space=pl.ANY)] * 3,
        out_specs=(
            pl.BlockSpec(memory_space=pltpu.VMEM),
            pl.BlockSpec(memory_space=pl.ANY),
            pl.BlockSpec(memory_space=pltpu.VMEM),
        ),
        scratch_shapes=[
            pltpu.VMEM((4, 4, tb, tb), bf),
            pltpu.VMEM((2, 2 * tb, hw), bf),
            pltpu.VMEM((2, 4, kr, hw), bf),
            pltpu.VMEM((2, 4 * tb, hw), bf),
            pltpu.VMEM((2, 4, tb, tb), bf),
            pltpu.VMEM((tb, tb), jnp.float32),
            pltpu.VMEM((2, 2, tb, hw), bf),
            pltpu.VMEM((2, 8, hw), jnp.float32),
            pltpu.VMEM((8, 8, hw), jnp.float32),
            dma((20,)), dma((16,)), dma((4,)), dma((4,)), dma((4,)), dma((8,)), dma((8,)),
            dma((2,)), dma((2,)), dma((4,)), dma((4,)), dma((8,)), dma((8,)),
        ],
        compiler_params=pltpu.CompilerParams(
            collective_id=0, has_side_effects=True, vmem_limit_bytes=48 * 1024 * 1024
        ),
    )(top_factor, masked, kid_factor)
    cross_cov = cross_half.astype(jnp.float32)
    onehot = (labels[:, :, None] == jnp.arange(G, dtype=jnp.int32)[None, None, :]).astype(
        jnp.float32
    )
    local_counts = jnp.sum(onehot, axis=(0, 1))
    label_sum, counts = lax.psum((jnp.einsum("kw,kwg->g", node_var, onehot), local_counts), "scol")
    return (top_cov, cross_cov, node_var, label_sum / counts)


def solution(mesh):
    placed = (
        P(("basin", "srow"), "scol"),
        P(("basin", "scol"), "srow", None),
        P(("basin", "scol"), "srow", None),
        P(("basin", "scol"), None),
        P(("basin", "scol"), None),
    )
    small = mesh.shape["srow"] == 4 and mesh.shape["scol"] == 4
    return jax.shard_map(
        per_device_fused if small else per_device,
        mesh=mesh,
        in_specs=placed,
        out_specs=(
            P(("basin", "srow"), "scol"),
            P(("basin", "scol"), "srow", None),
            P(("basin", "scol"), None),
            P("basin"),
        ),
        check_vma=False,
    )
```

```python
import jax
import jax.numpy as jnp
from jax import lax
from jax.experimental import pallas as pl
from jax.experimental.pallas import tpu as pltpu
from jax.sharding import PartitionSpec as P

RB = 128
G = 32


def per_device(top_inv, off_block, kid_inv, row_struct, labels):
    row_rank = lax.axis_index("srow")
    col_rank = lax.axis_index("scol")
    rows_top = top_inv.shape[0]
    cols_top = top_inv.shape[1]
    row_ids = row_rank * rows_top + jnp.arange(rows_top, dtype=jnp.int32)
    col_ids = col_rank * cols_top + jnp.arange(cols_top, dtype=jnp.int32)
    diagonal_one = (col_ids[None, :] == row_ids[:, None]).astype(top_inv.dtype)
    top_factor = jnp.where(col_ids[None, :] > row_ids[:, None], top_inv, diagonal_one)
    top_panel = lax.all_gather(top_factor, "srow", axis=0, tiled=True)
    block_sum = lax.psum_scatter(
        lax.dot_general(
            top_panel, top_factor, (((1,), (1,)), ((), ())), preferred_element_type=jnp.float32
        ),
        "scol",
        scatter_dimension=0,
        tiled=True,
    )
    top_cov = block_sum.T
    top_half = lax.all_gather(top_cov.astype(jnp.bfloat16), "scol", axis=1, tiled=True)
    kid_rows = kid_inv.shape[1]
    width = kid_inv.shape[2]
    kid_row_ids = row_rank * kid_rows + jnp.arange(kid_rows, dtype=jnp.int32)
    kid_col_ids = jnp.arange(width, dtype=jnp.int32)
    kid_one = (kid_row_ids[:, None] == kid_col_ids[None, :]).astype(kid_inv.dtype)
    kid_factor = jnp.where(kid_row_ids[:, None] > kid_col_ids[None, :], kid_inv, kid_one)
    local_rows = off_block.shape[1]
    block_ids = (row_rank * local_rows + jnp.arange(local_rows, dtype=jnp.int32)) // RB
    block_hits = (
        block_ids[:, None] == jnp.arange(row_struct.shape[1], dtype=jnp.int32)[None, :]
    ).astype(jnp.int32)
    kept_rows = jnp.sum(row_struct[:, None, :] * block_hits[None, :, :], axis=2)
    masked = jnp.where(kept_rows[:, :, None] != 0, off_block, jnp.zeros_like(off_block))
    product = jnp.einsum(
        "kac,kcw->kaw",
        masked,
        lax.all_gather(kid_factor, "srow", axis=1, tiled=True),
        preferred_element_type=jnp.float32,
    ).astype(jnp.bfloat16)
    image_sum = jnp.einsum(
        "am,kmw->kaw",
        top_half,
        lax.all_gather(product, "srow", axis=1, tiled=True),
        preferred_element_type=jnp.float32,
    )
    cross_cov = -image_sum
    own_part = jnp.sum(jnp.square(kid_factor.astype(jnp.float32)), axis=1) - jnp.sum(
        product.astype(jnp.float32) * cross_cov, axis=1
    )
    node_var = lax.psum(own_part, "srow")
    onehot = (labels[:, :, None] == jnp.arange(G, dtype=jnp.int32)[None, None, :]).astype(
        jnp.float32
    )
    local_counts = jnp.sum(onehot, axis=(0, 1))
    label_sum, counts = lax.psum((jnp.einsum("kw,kwg->g", node_var, onehot), local_counts), "scol")
    basin_var = label_sum / counts
    return (top_cov, cross_cov, node_var, basin_var)

MESH = pl.DeviceIdType.MESH


def dot(a, b, b_dim):
    return lax.dot_general(a, b, (((1,), (b_dim,)), ((), ())), preferred_element_type=jnp.float32)


def fused(f_ref, off_ref, kid_ref, keep_ref, cov_ref, cross_ref, var_ref,
          fall, offb, kidf, prod, th, acc, cbuf, vsum, vgot, kept,
          f_send, f_recv, off_send, off_recv, kid_send, kid_fwd, kid_recv,
          p_send, p_recv, c_send, c_recv, v_send, v_recv, k_send, k_recv):
    b, z, d = lax.axis_index("basin"), lax.axis_index("srow"), lax.axis_index("scol")
    h = lax.rem(d, 2)
    base = d - h
    sib = d + 1 - 2 * h
    across = lax.rem(d + 2, 4)
    far = lax.rem(sib + 2, 4)
    tb = f_ref.shape[0]
    kr = kid_ref.shape[1]
    hw = kid_ref.shape[2] // 2
    keeper = lax.div(z, 2)
    slot = lax.rem(z, 2)
    home = base + keeper
    is_keeper = h == keeper
    pending = []

    barrier = pltpu.get_barrier_semaphore()
    for s in range(1, 16):
        other = lax.rem(z * 4 + d + s, 16)
        pl.semaphore_signal(
            barrier, inc=1, device_id=(b, lax.div(other, 4), lax.rem(other, 4)), device_id_type=MESH
        )
    pl.semaphore_wait(barrier, 15)

    def send(cond, source, target, ssem, rsem, zz, cc):
        copy = pltpu.make_async_remote_copy(
            src_ref=source, dst_ref=target, send_sem=ssem, recv_sem=rsem,
            device_id=(b, zz, cc), device_id_type=MESH,
        )
        pl.when(cond)(lambda: copy.start())
        pending.append((cond, copy))

    def local(cond, source, target, rsem):
        pl.when(cond)(lambda: pltpu.make_async_copy(source, target, rsem).start())

    def arrived(cond, target, rsem):
        pl.when(cond)(lambda: pltpu.make_async_copy(target, target, rsem).wait())

    def fan(s, r, source):
        have = r <= d
        target, rsem = fall.at[r, d], f_recv.at[r * 4 + d]
        send(have & (r <= z) & (z < 3), source, target, f_send.at[s * 5], rsem, jnp.minimum(z + 1, 3), d)
        send(have & (r >= z) & (z > 0), source, target, f_send.at[s * 5 + 1], rsem, jnp.maximum(z - 1, 0), d)
        send(have, source, target, f_send.at[s * 5 + 2], rsem, z, across)
        send(have, source, target, f_send.at[s * 5 + 3], rsem, z, sib)

    order = (z, z + 1 - 2 * slot, jnp.where(z < 2, 2, 1), jnp.where(z < 2, 3, 0))
    local(z <= d, f_ref, fall.at[z, d], f_recv.at[z * 4 + d])
    fan(0, z, f_ref)

    def start_inputs(part):
        cols = pl.ds(part * hw, hw)
        needed = (z >= 2) if part else (z >= 0)
        spot = pl.ds(pl.multiple_of(slot * tb, tb), tb)
        for i in range(2):
            kid = 2 * h + i
            n = part * 2 + i
            send((kid != z) & needed, kid_ref.at[i, :, cols], kidf.at[part, z],
                 kid_send.at[n], kid_recv.at[part * 4 + z], kid, d)
            local((kid == z) & needed, kid_ref.at[i, :, cols], kidf.at[part, z], kid_recv.at[part * 4 + z])
            send(kid != z, off_ref.at[i, :, cols], offb.at[part, spot, :],
                 off_send.at[n], off_recv.at[part * 2 + slot], kid, home)
            local(kid == z, off_ref.at[i, :, cols], offb.at[part, spot, :], off_recv.at[part * 2 + slot])

    start_inputs(1)
    send(is_keeper, keep_ref.at[slot], kept, k_send.at[0], k_recv.at[0], z, sib)
    local(is_keeper, keep_ref.at[slot], kept, k_recv.at[0])

    def pass_on(s):
        r = order[s]
        arrived(r <= across, fall.at[r, across], f_recv.at[r * 4 + across])
        send(r <= across, fall.at[r, across], fall.at[r, across], f_send.at[s * 5 + 4],
             f_recv.at[r * 4 + across], z, sib)

    for s in range(1, 4):
        r = order[s]
        arrived(r <= d, fall.at[r, d], f_recv.at[r * 4 + d])
        fan(s, r, fall.at[r, d])
        pass_on(s - 1)
    pass_on(3)
    start_inputs(0)
    arrived(z >= 0, kept, k_recv.at[0])
    def outer_block(r, c):
        acc[...] = jnp.zeros_like(acc)

        @pl.loop(jnp.maximum(r, c), 4)
        def _(k):
            acc[...] += dot(fall[r, k], fall[c, k], 1)

    half = pl.multiple_of(h * 2 * tb, 2 * tb)
    def make_product(part):
        low = 2 if part else 0
        for zp in range(low, 4):
            arrived(z >= 0, kidf.at[part, zp], kid_recv.at[part * 4 + zp])
            send(is_keeper, kidf.at[part, zp], kidf.at[part, zp], kid_fwd.at[part * 4 + zp],
                 kid_recv.at[part * 4 + zp], z, sib)
        for q in range(2):
            arrived(z >= 0, offb.at[part, pl.ds(q * tb, tb), :], off_recv.at[part * 2 + q])

        @pl.loop(0, 2 * tb // 256)
        def _(m):
            rows = pl.ds(pl.multiple_of(m * 256, 256), 256)
            lower = kidf[part, 2:4].reshape(2 * kr, hw)
            total = dot(offb[1, rows, :], lower, 0)
            if part == 0:
                total += dot(offb[0, rows, :], kidf[0, 0:2].reshape(2 * kr, hw), 0)
            for t in range(2):
                cut = total[t * RB:(t + 1) * RB] * kept[h * 8 + m * 2 + t][0:1]
                prod[part, pl.ds(pl.multiple_of(half + m * 256 + t * RB, RB), RB), :] = cut.astype(jnp.bfloat16)

        mine = prod.at[part, pl.ds(half, 2 * tb), :]
        send(z >= 0, mine, mine, p_send.at[part], p_recv.at[part], z, sib)

        vsum[part] = jnp.zeros((8, hw), jnp.float32)

        @pl.when(h == 0)
        def _():
            for zp in range(low, 4):
                square = jnp.square(kidf[part, zp].astype(jnp.float32))
                vsum[part] += jnp.sum(square.reshape(kr // 8, 8, hw), axis=0)

    def make_cross(part):
        cols = pl.ds(part * hw, hw)
        theirs = prod.at[part, pl.ds(pl.multiple_of((1 - h) * 2 * tb, 2 * tb), 2 * tb), :]
        arrived(z >= 0, theirs, p_recv.at[part])
        for i in range(2):
            for m in range(2):
                rows = pl.ds(m * (tb // 2), tb // 2)
                total = dot(th[i, 0, rows, :], prod[part, 0:tb, :], 0)
                for j in range(1, 4):
                    total += dot(th[i, j, rows, :], prod[part, j * tb:(j + 1) * tb, :], 0)
                own = prod[part, pl.ds(pl.multiple_of(half + i * tb + m * (tb // 2), tb // 2), tb // 2), :]
                vsum[part] += jnp.sum((own.astype(jnp.float32) * total).reshape(tb // 16, 8, hw), axis=0)
                cbuf[part, i, rows, :] = (-total).astype(jnp.bfloat16)
            there = 2 * h + i
            send(there != z, cbuf.at[part, i], cross_ref.at[slot, :, cols], c_send.at[part * 2 + i],
                 c_recv.at[part * 2 + slot], there, home)
            local(there == z, cbuf.at[part, i], cross_ref.at[slot, :, cols], c_recv.at[part * 2 + slot])
        for there in range(4):
            to_self = (there == z) & is_keeper
            place = part * 4 + slot * 2 + h
            send(jnp.logical_not(to_self), vsum.at[part], vgot.at[place], v_send.at[part * 4 + there],
                 v_recv.at[place], there, home)
            local(to_self, vsum.at[part], vgot.at[place], v_recv.at[place])

    make_product(1)
    arrived(z <= d, fall.at[z, d], f_recv.at[z * 4 + d])
    for s in range(4):
        for c in (sib, far):
            arrived(order[s] <= c, fall.at[order[s], c], f_recv.at[order[s] * 4 + c])

    @pl.loop(0, 8)
    def _(n):
        i, j = lax.div(n, 4), lax.rem(n, 4)
        outer_block(2 * h + i, j)
        th[i, j] = acc[...].astype(jnp.bfloat16)

    make_cross(1)
    make_product(0)
    make_cross(0)
    outer_block(z, d)
    cov_ref[...] = acc[...]

    for part in (1, 0):
        cols = pl.ds(part * hw, hw)
        for q in range(2):
            for hh in range(2):
                arrived(z >= 0, vgot.at[part * 4 + q * 2 + hh], v_recv.at[part * 4 + q * 2 + hh])
            both = vgot[part * 4 + q * 2] + vgot[part * 4 + q * 2 + 1]
            var_ref[q:q + 1, cols] = jnp.sum(both, axis=0, keepdims=True)
    for part in (1, 0):
        for q in range(2):
            place = cross_ref.at[q, :, pl.ds(part * hw, hw)]
            arrived(z >= 0, place, c_recv.at[part * 2 + q])
    for cond, copy in pending:
        pl.when(cond)(copy.wait_send)


def per_device_fused(top_inv, off_block, kid_inv, row_struct, labels):
    row_rank = lax.axis_index("srow")
    col_rank = lax.axis_index("scol")
    tb = top_inv.shape[0]
    row_ids = row_rank * tb + jnp.arange(tb, dtype=jnp.int32)
    col_ids = col_rank * tb + jnp.arange(tb, dtype=jnp.int32)
    diagonal_one = (col_ids[None, :] == row_ids[:, None]).astype(top_inv.dtype)
    top_factor = jnp.where(col_ids[None, :] > row_ids[:, None], top_inv, diagonal_one)
    kr = kid_inv.shape[1]
    width = kid_inv.shape[2]
    hw = width // 2
    kid_row_ids = row_rank * kr + jnp.arange(kr, dtype=jnp.int32)
    kid_col_ids = jnp.arange(width, dtype=jnp.int32)
    kid_one = (kid_row_ids[:, None] == kid_col_ids[None, :]).astype(kid_inv.dtype)
    kid_factor = jnp.where(kid_row_ids[:, None] > kid_col_ids[None, :], kid_inv, kid_one)
    keep = jnp.broadcast_to(
        (row_struct != 0).astype(jnp.float32)[:, :, None, None], row_struct.shape + (8, hw)
    )
    bf = jnp.bfloat16
    dma = pltpu.SemaphoreType.DMA
    top_cov, cross_half, node_var = pl.pallas_call(
        fused,
        out_shape=(
            jax.ShapeDtypeStruct((tb, tb), jnp.float32),
            jax.ShapeDtypeStruct((2, tb, width), bf),
            jax.ShapeDtypeStruct((2, width), jnp.float32),
        ),
        in_specs=[pl.BlockSpec(memory_space=pl.ANY)] * 4,
        out_specs=(
            pl.BlockSpec(memory_space=pltpu.VMEM),
            pl.BlockSpec(memory_space=pl.ANY),
            pl.BlockSpec(memory_space=pltpu.VMEM),
        ),
        scratch_shapes=[
            pltpu.VMEM((4, 4, tb, tb), bf),
            pltpu.VMEM((2, 2 * tb, hw), bf),
            pltpu.VMEM((2, 4, kr, hw), bf),
            pltpu.VMEM((2, 4 * tb, hw), bf),
            pltpu.VMEM((2, 4, tb, tb), bf),
            pltpu.VMEM((tb, tb), jnp.float32),
            pltpu.VMEM((2, 2, tb, hw), bf),
            pltpu.VMEM((2, 8, hw), jnp.float32),
            pltpu.VMEM((8, 8, hw), jnp.float32),
            pltpu.VMEM((row_struct.shape[1], 8, hw), jnp.float32),
            dma((20,)), dma((16,)), dma((4,)), dma((4,)), dma((4,)), dma((8,)), dma((8,)),
            dma((2,)), dma((2,)), dma((4,)), dma((4,)), dma((8,)), dma((8,)),
            dma((1,)), dma((1,)),
        ],
        compiler_params=pltpu.CompilerParams(
            collective_id=0, has_side_effects=True, vmem_limit_bytes=48 * 1024 * 1024
        ),
    )(top_factor, off_block, kid_factor, keep)
    cross_cov = cross_half.astype(jnp.float32)
    onehot = (labels[:, :, None] == jnp.arange(G, dtype=jnp.int32)[None, None, :]).astype(
        jnp.float32
    )
    local_counts = jnp.sum(onehot, axis=(0, 1))
    label_sum, counts = lax.psum((jnp.einsum("kw,kwg->g", node_var, onehot), local_counts), "scol")
    return (top_cov, cross_cov, node_var, label_sum / counts)


def solution(mesh):
    placed = (
        P(("basin", "srow"), "scol"),
        P(("basin", "scol"), "srow", None),
        P(("basin", "scol"), "srow", None),
        P(("basin", "scol"), None),
        P(("basin", "scol"), None),
    )
    small = mesh.shape["srow"] == 4 and mesh.shape["scol"] == 4
    return jax.shard_map(
        per_device_fused if small else per_device,
        mesh=mesh,
        in_specs=placed,
        out_specs=(
            P(("basin", "srow"), "scol"),
            P(("basin", "scol"), "srow", None),
            P(("basin", "scol"), None),
            P("basin"),
        ),
        check_vma=False,
    )
```

```python
import jax
import jax.numpy as jnp
from jax import lax
from jax.experimental import pallas as pl
from jax.experimental.pallas import tpu as pltpu
from jax.sharding import PartitionSpec as P

RB = 128
G = 32


def per_device(top_inv, off_block, kid_inv, row_struct, labels):
    row_rank = lax.axis_index("srow")
    col_rank = lax.axis_index("scol")
    rows_top = top_inv.shape[0]
    cols_top = top_inv.shape[1]
    row_ids = row_rank * rows_top + jnp.arange(rows_top, dtype=jnp.int32)
    col_ids = col_rank * cols_top + jnp.arange(cols_top, dtype=jnp.int32)
    diagonal_one = (col_ids[None, :] == row_ids[:, None]).astype(top_inv.dtype)
    top_factor = jnp.where(col_ids[None, :] > row_ids[:, None], top_inv, diagonal_one)
    top_panel = lax.all_gather(top_factor, "srow", axis=0, tiled=True)
    block_sum = lax.psum_scatter(
        lax.dot_general(
            top_panel, top_factor, (((1,), (1,)), ((), ())), preferred_element_type=jnp.float32
        ),
        "scol",
        scatter_dimension=0,
        tiled=True,
    )
    top_cov = block_sum.T
    top_half = lax.all_gather(top_cov.astype(jnp.bfloat16), "scol", axis=1, tiled=True)
    kid_rows = kid_inv.shape[1]
    width = kid_inv.shape[2]
    kid_row_ids = row_rank * kid_rows + jnp.arange(kid_rows, dtype=jnp.int32)
    kid_col_ids = jnp.arange(width, dtype=jnp.int32)
    kid_one = (kid_row_ids[:, None] == kid_col_ids[None, :]).astype(kid_inv.dtype)
    kid_factor = jnp.where(kid_row_ids[:, None] > kid_col_ids[None, :], kid_inv, kid_one)
    local_rows = off_block.shape[1]
    block_ids = (row_rank * local_rows + jnp.arange(local_rows, dtype=jnp.int32)) // RB
    block_hits = (
        block_ids[:, None] == jnp.arange(row_struct.shape[1], dtype=jnp.int32)[None, :]
    ).astype(jnp.int32)
    kept_rows = jnp.sum(row_struct[:, None, :] * block_hits[None, :, :], axis=2)
    masked = jnp.where(kept_rows[:, :, None] != 0, off_block, jnp.zeros_like(off_block))
    product = jnp.einsum(
        "kac,kcw->kaw",
        masked,
        lax.all_gather(kid_factor, "srow", axis=1, tiled=True),
        preferred_element_type=jnp.float32,
    ).astype(jnp.bfloat16)
    image_sum = jnp.einsum(
        "am,kmw->kaw",
        top_half,
        lax.all_gather(product, "srow", axis=1, tiled=True),
        preferred_element_type=jnp.float32,
    )
    cross_cov = -image_sum
    own_part = jnp.sum(jnp.square(kid_factor.astype(jnp.float32)), axis=1) - jnp.sum(
        product.astype(jnp.float32) * cross_cov, axis=1
    )
    node_var = lax.psum(own_part, "srow")
    onehot = (labels[:, :, None] == jnp.arange(G, dtype=jnp.int32)[None, None, :]).astype(
        jnp.float32
    )
    local_counts = jnp.sum(onehot, axis=(0, 1))
    label_sum, counts = lax.psum((jnp.einsum("kw,kwg->g", node_var, onehot), local_counts), "scol")
    basin_var = label_sum / counts
    return (top_cov, cross_cov, node_var, basin_var)

MESH = pl.DeviceIdType.MESH


def dot(a, b, b_dim):
    return lax.dot_general(a, b, (((1,), (b_dim,)), ((), ())), preferred_element_type=jnp.float32)


def fused(f_ref, off_ref, kid_ref, keep_ref, lab_ref, cov_ref, cross_ref, var_ref, mean_ref,
          fall, offb, kidf, prod, th, acc, cbuf, vsum, vgot, kept, tally,
          f_send, f_recv, off_send, off_recv, kid_send, kid_fwd, kid_recv,
          p_send, p_recv, c_send, c_recv, v_send, v_recv, k_send, k_recv, t_send, t_recv):
    b, z, d = lax.axis_index("basin"), lax.axis_index("srow"), lax.axis_index("scol")
    h = lax.rem(d, 2)
    base = d - h
    sib = d + 1 - 2 * h
    across = lax.rem(d + 2, 4)
    far = lax.rem(sib + 2, 4)
    tb = f_ref.shape[0]
    kr = kid_ref.shape[1]
    hw = kid_ref.shape[2] // 2
    keeper = lax.div(z, 2)
    slot = lax.rem(z, 2)
    home = base + keeper
    is_keeper = h == keeper
    pending = []

    def kid_view(part, zp):
        return kidf.at[part, zp, :, pl.ds(0, hw // 2 if zp == 2 * part else hw)]

    for part in (0, 1):
        kidf[part, 2 * part, :, hw // 2:] = jnp.zeros((kr, hw - hw // 2), kidf.dtype)

    barrier = pltpu.get_barrier_semaphore()
    for s in range(1, 16):
        other = lax.rem(z * 4 + d + s, 16)
        pl.semaphore_signal(
            barrier, inc=1, device_id=(b, lax.div(other, 4), lax.rem(other, 4)), device_id_type=MESH
        )
    pl.semaphore_wait(barrier, 15)

    def send(cond, source, target, ssem, rsem, zz, cc):
        copy = pltpu.make_async_remote_copy(
            src_ref=source, dst_ref=target, send_sem=ssem, recv_sem=rsem,
            device_id=(b, zz, cc), device_id_type=MESH,
        )
        pl.when(cond)(lambda: copy.start())
        pending.append((cond, copy))

    def local(cond, source, target, rsem):
        pl.when(cond)(lambda: pltpu.make_async_copy(source, target, rsem).start())

    def arrived(cond, target, rsem):
        pl.when(cond)(lambda: pltpu.make_async_copy(target, target, rsem).wait())

    def columns(r):
        moved = (r == 3) & (z < 3)
        return jnp.where(moved, across, d), jnp.where(moved, d, across)

    def fan(s, r, source):
        c, _ = columns(r)
        have = r <= c
        target, rsem = fall.at[r, c], f_recv.at[r * 4 + c]
        send(have & (r <= z) & (z < 3), source, target, f_send.at[s * 6], rsem, jnp.minimum(z + 1, 3), d)
        send(have & (r >= z) & (z > 0) & (z < 3), source, target, f_send.at[s * 6 + 1], rsem,
             jnp.maximum(z - 1, 0), d)
        send(have, source, target, f_send.at[s * 6 + 2], rsem, z, across)
        send(have, source, target, f_send.at[s * 6 + 3], rsem, z, sib)

    order = (z, z + 1 - 2 * slot, jnp.where(z < 2, 2, 1), jnp.where(z < 2, 3, 0))
    local(z <= d, f_ref, fall.at[z, d], f_recv.at[z * 4 + d])
    fan(0, z, f_ref)

    def start_inputs(part):
        cols = pl.ds(part * hw, hw)
        needed = (z >= 2) if part else (z >= 0)
        spot = pl.ds(pl.multiple_of(slot * tb, tb), tb)
        for i in range(2):
            kid = 2 * h + i
            n = part * 2 + i
            for narrow in (True, False):
                width = hw // 2 if narrow else hw
                chosen = needed & ((z == 2 * part) if narrow else (z != 2 * part))
                source = kid_ref.at[i, :, pl.ds(part * hw, width)]
                target = kidf.at[part, z, :, pl.ds(0, width)]
                send((kid != z) & chosen, source, target, kid_send.at[n], kid_recv.at[part * 4 + z], kid, d)
                local((kid == z) & chosen, source, target, kid_recv.at[part * 4 + z])
            send(kid != z, off_ref.at[i, :, cols], offb.at[part, spot, :],
                 off_send.at[n], off_recv.at[part * 2 + slot], kid, home)
            local(kid == z, off_ref.at[i, :, cols], offb.at[part, spot, :], off_recv.at[part * 2 + slot])

    start_inputs(1)
    send(is_keeper, keep_ref.at[slot], kept, k_send.at[0], k_recv.at[0], z, sib)
    local(is_keeper, keep_ref.at[slot], kept, k_recv.at[0])

    def pass_on(s):
        r = order[s]
        _, c = columns(r)
        target, rsem = fall.at[r, c], f_recv.at[r * 4 + c]
        arrived(r <= c, target, rsem)
        send(r <= c, target, target, f_send.at[s * 6 + 4], rsem, z, sib)
        send((r <= c) & (r == 3) & (z == 3), target, target, f_send.at[s * 6 + 5], rsem,
             jnp.maximum(z - 1, 0), d)

    for s in range(1, 4):
        pass_on(s - 1)
        r = order[s]
        c, _ = columns(r)
        arrived(r <= c, fall.at[r, c], f_recv.at[r * 4 + c])
        fan(s, r, fall.at[r, c])
    pass_on(3)
    start_inputs(0)
    arrived(z >= 0, kept, k_recv.at[0])
    def outer_block(r, c):
        acc[...] = jnp.zeros_like(acc)

        @pl.loop(jnp.maximum(r, c), 4)
        def _(k):
            acc[...] += dot(fall[r, k], fall[c, k], 1)

    half = pl.multiple_of(h * 2 * tb, 2 * tb)
    def make_product(part):
        low = 2 if part else 0
        for zp in range(low, 4):
            view = kid_view(part, zp)
            arrived(z >= 0, view, kid_recv.at[part * 4 + zp])
            send(is_keeper, view, view, kid_fwd.at[part * 4 + zp],
                 kid_recv.at[part * 4 + zp], z, sib)
        for q in range(2):
            arrived(z >= 0, offb.at[part, pl.ds(q * tb, tb), :], off_recv.at[part * 2 + q])

        @pl.loop(0, 2 * tb // 256)
        def _(m):
            rows = pl.ds(pl.multiple_of(m * 256, 256), 256)
            lower = kidf[part, 2:4].reshape(2 * kr, hw)
            total = dot(offb[1, rows, :], lower, 0)
            if part == 0:
                total += dot(offb[0, rows, :], kidf[0, 0:2].reshape(2 * kr, hw), 0)
            for t in range(2):
                cut = total[t * RB:(t + 1) * RB] * kept[h * 8 + m * 2 + t][0:1]
                prod[part, pl.ds(pl.multiple_of(half + m * 256 + t * RB, RB), RB), :] = cut.astype(jnp.bfloat16)

        mine = prod.at[part, pl.ds(half, 2 * tb), :]
        send(z >= 0, mine, mine, p_send.at[part], p_recv.at[part], z, sib)

        vsum[part] = jnp.zeros((8, hw), jnp.float32)

        @pl.when(h == 0)
        def _():
            for zp in range(low, 4):
                square = jnp.square(kidf[part, zp].astype(jnp.float32))
                vsum[part] += jnp.sum(square.reshape(kr // 8, 8, hw), axis=0)

    def make_cross(part):
        cols = pl.ds(part * hw, hw)
        theirs = prod.at[part, pl.ds(pl.multiple_of((1 - h) * 2 * tb, 2 * tb), 2 * tb), :]
        arrived(z >= 0, theirs, p_recv.at[part])
        for i in range(2):
            for m in range(2):
                rows = pl.ds(m * (tb // 2), tb // 2)
                total = dot(th[i, 0, rows, :], prod[part, 0:tb, :], 0)
                for j in range(1, 4):
                    total += dot(th[i, j, rows, :], prod[part, j * tb:(j + 1) * tb, :], 0)
                own = prod[part, pl.ds(pl.multiple_of(half + i * tb + m * (tb // 2), tb // 2), tb // 2), :]
                vsum[part] += jnp.sum((own.astype(jnp.float32) * total).reshape(tb // 16, 8, hw), axis=0)
                cbuf[part, i, rows, :] = (-total).astype(jnp.bfloat16)
            there = 2 * h + i
            send(there != z, cbuf.at[part, i], cross_ref.at[slot, :, cols], c_send.at[part * 2 + i],
                 c_recv.at[part * 2 + slot], there, home)
            local(there == z, cbuf.at[part, i], cross_ref.at[slot, :, cols], c_recv.at[part * 2 + slot])
        for there in range(4):
            to_self = (there == z) & is_keeper
            place = part * 4 + slot * 2 + h
            send(jnp.logical_not(to_self), vsum.at[part], vgot.at[place], v_send.at[part * 4 + there],
                 v_recv.at[place], there, home)
            local(to_self, vsum.at[part], vgot.at[place], v_recv.at[place])

    make_product(1)
    arrived(z <= d, fall.at[z, d], f_recv.at[z * 4 + d])
    for s in range(4):
        for c in (sib, far):
            arrived(order[s] <= c, fall.at[order[s], c], f_recv.at[order[s] * 4 + c])

    @pl.loop(0, 8)
    def _(n):
        i, j = lax.div(n, 4), lax.rem(n, 4)
        outer_block(2 * h + i, j)
        th[i, j] = acc[...].astype(jnp.bfloat16)

    make_cross(1)
    make_product(0)
    make_cross(0)
    outer_block(z, d)
    cov_ref[...] = acc[...]

    for part in (1, 0):
        cols = pl.ds(part * hw, hw)
        for q in range(2):
            for hh in range(2):
                arrived(z >= 0, vgot.at[part * 4 + q * 2 + hh], v_recv.at[part * 4 + q * 2 + hh])
            both = vgot[part * 4 + q * 2] + vgot[part * 4 + q * 2 + 1]
            var_ref[q:q + 1, cols] = jnp.sum(both, axis=0, keepdims=True)
    groups = lax.broadcasted_iota(jnp.int32, (G, 2 * hw), 0)
    sums = jnp.zeros((G, 128), jnp.float32)
    counts = jnp.zeros((G, 128), jnp.float32)
    for q in range(2):
        hit = groups == lab_ref[q:q + 1, :]
        terms = jnp.where(hit, var_ref[q:q + 1, :], 0.0)
        ones = jnp.where(hit, 1.0, 0.0)
        for t in range(2 * hw // 128):
            sums += terms[:, t * 128:(t + 1) * 128]
            counts += ones[:, t * 128:(t + 1) * 128]
    tally[d, 0] = sums
    tally[d, 1] = counts
    for n, c in enumerate((sib, across, far)):
        send(z >= 0, tally.at[d], tally.at[d], t_send.at[n], t_recv.at[d], z, c)
    for c in (sib, across, far):
        arrived(z >= 0, tally.at[c], t_recv.at[c])
    sums = tally[0, 0] + tally[1, 0] + tally[2, 0] + tally[3, 0]
    counts = tally[0, 1] + tally[1, 1] + tally[2, 1] + tally[3, 1]
    mean = jnp.sum(sums, axis=1, keepdims=True) / jnp.sum(counts, axis=1, keepdims=True)
    mean_ref[...] = jnp.broadcast_to(mean, mean_ref.shape)
    for part in (1, 0):
        for q in range(2):
            place = cross_ref.at[q, :, pl.ds(part * hw, hw)]
            arrived(z >= 0, place, c_recv.at[part * 2 + q])
    for cond, copy in pending:
        pl.when(cond)(copy.wait_send)


def per_device_fused(top_inv, off_block, kid_inv, row_struct, labels):
    row_rank = lax.axis_index("srow")
    col_rank = lax.axis_index("scol")
    tb = top_inv.shape[0]
    row_ids = row_rank * tb + jnp.arange(tb, dtype=jnp.int32)
    col_ids = col_rank * tb + jnp.arange(tb, dtype=jnp.int32)
    diagonal_one = (col_ids[None, :] == row_ids[:, None]).astype(top_inv.dtype)
    top_factor = jnp.where(col_ids[None, :] > row_ids[:, None], top_inv, diagonal_one)
    kr = kid_inv.shape[1]
    width = kid_inv.shape[2]
    hw = width // 2
    kid_row_ids = row_rank * kr + jnp.arange(kr, dtype=jnp.int32)
    kid_col_ids = jnp.arange(width, dtype=jnp.int32)
    kid_one = (kid_row_ids[:, None] == kid_col_ids[None, :]).astype(kid_inv.dtype)
    kid_factor = jnp.where(kid_row_ids[:, None] > kid_col_ids[None, :], kid_inv, kid_one)
    keep = jnp.broadcast_to(
        (row_struct != 0).astype(jnp.float32)[:, :, None, None], row_struct.shape + (8, hw)
    )
    bf = jnp.bfloat16
    dma = pltpu.SemaphoreType.DMA
    top_cov, cross_half, node_var, means = pl.pallas_call(
        fused,
        out_shape=(
            jax.ShapeDtypeStruct((tb, tb), jnp.float32),
            jax.ShapeDtypeStruct((2, tb, width), bf),
            jax.ShapeDtypeStruct((2, width), jnp.float32),
            jax.ShapeDtypeStruct((G, 128), jnp.float32),
        ),
        in_specs=[pl.BlockSpec(memory_space=pl.ANY)] * 4 + [pl.BlockSpec(memory_space=pltpu.VMEM)],
        out_specs=(
            pl.BlockSpec(memory_space=pltpu.VMEM),
            pl.BlockSpec(memory_space=pl.ANY),
            pl.BlockSpec(memory_space=pltpu.VMEM),
            pl.BlockSpec(memory_space=pltpu.VMEM),
        ),
        scratch_shapes=[
            pltpu.VMEM((4, 4, tb, tb), bf),
            pltpu.VMEM((2, 2 * tb, hw), bf),
            pltpu.VMEM((2, 4, kr, hw), bf),
            pltpu.VMEM((2, 4 * tb, hw), bf),
            pltpu.VMEM((2, 4, tb, tb), bf),
            pltpu.VMEM((tb, tb), jnp.float32),
            pltpu.VMEM((2, 2, tb, hw), bf),
            pltpu.VMEM((2, 8, hw), jnp.float32),
            pltpu.VMEM((8, 8, hw), jnp.float32),
            pltpu.VMEM((row_struct.shape[1], 8, hw), jnp.float32),
            pltpu.VMEM((4, 2, G, 128), jnp.float32),
            dma((24,)), dma((16,)), dma((4,)), dma((4,)), dma((4,)), dma((8,)), dma((8,)),
            dma((2,)), dma((2,)), dma((4,)), dma((4,)), dma((8,)), dma((8,)),
            dma((1,)), dma((1,)), dma((3,)), dma((4,)),
        ],
        compiler_params=pltpu.CompilerParams(
            collective_id=0, has_side_effects=True, vmem_limit_bytes=48 * 1024 * 1024
        ),
    )(top_factor, off_block, kid_factor, keep, labels)
    return (top_cov, cross_half.astype(jnp.float32), node_var, means[:, 0])


def solution(mesh):
    placed = (
        P(("basin", "srow"), "scol"),
        P(("basin", "scol"), "srow", None),
        P(("basin", "scol"), "srow", None),
        P(("basin", "scol"), None),
        P(("basin", "scol"), None),
    )
    small = mesh.shape["srow"] == 4 and mesh.shape["scol"] == 4
    return jax.shard_map(
        per_device_fused if small else per_device,
        mesh=mesh,
        in_specs=placed,
        out_specs=(
            P(("basin", "srow"), "scol"),
            P(("basin", "scol"), "srow", None),
            P(("basin", "scol"), None),
            P("basin"),
        ),
        check_vma=False,
    )
```

```python
import jax
import jax.numpy as jnp
from jax import lax
from jax.experimental import pallas as pl
from jax.experimental.pallas import tpu as pltpu
from jax.sharding import PartitionSpec as P

RB = 128
G = 32


def per_device(top_inv, off_block, kid_inv, row_struct, labels):
    row_rank = lax.axis_index("srow")
    col_rank = lax.axis_index("scol")
    rows_top = top_inv.shape[0]
    cols_top = top_inv.shape[1]
    row_ids = row_rank * rows_top + jnp.arange(rows_top, dtype=jnp.int32)
    col_ids = col_rank * cols_top + jnp.arange(cols_top, dtype=jnp.int32)
    diagonal_one = (col_ids[None, :] == row_ids[:, None]).astype(top_inv.dtype)
    top_factor = jnp.where(col_ids[None, :] > row_ids[:, None], top_inv, diagonal_one)
    top_panel = lax.all_gather(top_factor, "srow", axis=0, tiled=True)
    block_sum = lax.psum_scatter(
        lax.dot_general(
            top_panel, top_factor, (((1,), (1,)), ((), ())), preferred_element_type=jnp.float32
        ),
        "scol",
        scatter_dimension=0,
        tiled=True,
    )
    top_cov = block_sum.T
    top_half = lax.all_gather(top_cov.astype(jnp.bfloat16), "scol", axis=1, tiled=True)
    kid_rows = kid_inv.shape[1]
    width = kid_inv.shape[2]
    kid_row_ids = row_rank * kid_rows + jnp.arange(kid_rows, dtype=jnp.int32)
    kid_col_ids = jnp.arange(width, dtype=jnp.int32)
    kid_one = (kid_row_ids[:, None] == kid_col_ids[None, :]).astype(kid_inv.dtype)
    kid_factor = jnp.where(kid_row_ids[:, None] > kid_col_ids[None, :], kid_inv, kid_one)
    local_rows = off_block.shape[1]
    block_ids = (row_rank * local_rows + jnp.arange(local_rows, dtype=jnp.int32)) // RB
    block_hits = (
        block_ids[:, None] == jnp.arange(row_struct.shape[1], dtype=jnp.int32)[None, :]
    ).astype(jnp.int32)
    kept_rows = jnp.sum(row_struct[:, None, :] * block_hits[None, :, :], axis=2)
    masked = jnp.where(kept_rows[:, :, None] != 0, off_block, jnp.zeros_like(off_block))
    product = jnp.einsum(
        "kac,kcw->kaw",
        masked,
        lax.all_gather(kid_factor, "srow", axis=1, tiled=True),
        preferred_element_type=jnp.float32,
    ).astype(jnp.bfloat16)
    image_sum = jnp.einsum(
        "am,kmw->kaw",
        top_half,
        lax.all_gather(product, "srow", axis=1, tiled=True),
        preferred_element_type=jnp.float32,
    )
    cross_cov = -image_sum
    own_part = jnp.sum(jnp.square(kid_factor.astype(jnp.float32)), axis=1) - jnp.sum(
        product.astype(jnp.float32) * cross_cov, axis=1
    )
    node_var = lax.psum(own_part, "srow")
    onehot = (labels[:, :, None] == jnp.arange(G, dtype=jnp.int32)[None, None, :]).astype(
        jnp.float32
    )
    local_counts = jnp.sum(onehot, axis=(0, 1))
    label_sum, counts = lax.psum((jnp.einsum("kw,kwg->g", node_var, onehot), local_counts), "scol")
    basin_var = label_sum / counts
    return (top_cov, cross_cov, node_var, basin_var)

MESH = pl.DeviceIdType.MESH


def dot(a, b, b_dim):
    return lax.dot_general(a, b, (((1,), (b_dim,)), ((), ())), preferred_element_type=jnp.float32)


def fused(f_ref, off_ref, kid_ref, keep_ref, lab_ref, cov_ref, cross_ref, var_ref, mean_ref,
          fall, offb, kidf, prod, th, acc, cbuf, vsum, vgot, kept, tally,
          f_send, f_recv, off_send, off_recv, kid_send, kid_fwd, kid_recv,
          p_send, p_recv, c_send, c_recv, v_send, v_recv, k_send, k_recv, t_send, t_recv):
    b, z, d = lax.axis_index("basin"), lax.axis_index("srow"), lax.axis_index("scol")
    h = lax.rem(d, 2)
    base = d - h
    sib = d + 1 - 2 * h
    across = lax.rem(d + 2, 4)
    far = lax.rem(sib + 2, 4)
    tb = f_ref.shape[0]
    kr = kid_ref.shape[1]
    hw = kid_ref.shape[2] // 2
    keeper = lax.div(z, 2)
    slot = lax.rem(z, 2)
    home = base + keeper
    is_keeper = h == keeper
    pending = []

    def kid_view(part, zp):
        return kidf.at[part, zp, :, pl.ds(0, hw // 2 if zp == 2 * part else hw)]

    for part in (0, 1):
        kidf[part, 2 * part, :, hw // 2:] = jnp.zeros((kr, hw - hw // 2), kidf.dtype)

    barrier = pltpu.get_barrier_semaphore()
    for s in range(1, 16):
        other = lax.rem(z * 4 + d + s, 16)
        pl.semaphore_signal(
            barrier, inc=1, device_id=(b, lax.div(other, 4), lax.rem(other, 4)), device_id_type=MESH
        )
    pl.semaphore_wait(barrier, 15)

    def send(cond, source, target, ssem, rsem, zz, cc):
        copy = pltpu.make_async_remote_copy(
            src_ref=source, dst_ref=target, send_sem=ssem, recv_sem=rsem,
            device_id=(b, zz, cc), device_id_type=MESH,
        )
        pl.when(cond)(lambda: copy.start())
        pending.append((cond, copy))

    def local(cond, source, target, rsem):
        pl.when(cond)(lambda: pltpu.make_async_copy(source, target, rsem).start())

    def arrived(cond, target, rsem):
        pl.when(cond)(lambda: pltpu.make_async_copy(target, target, rsem).wait())

    def columns(r):
        moved = (r == 3) & (z < 3)
        return jnp.where(moved, across, d), jnp.where(moved, d, across)

    def fan(s, r, source):
        c, _ = columns(r)
        have = r <= c
        target, rsem = fall.at[r, c], f_recv.at[r * 4 + c]
        send(have & (r <= z) & (z < 3), source, target, f_send.at[s * 6], rsem, jnp.minimum(z + 1, 3), d)
        send(have & (r >= z) & (z > 0) & (z < 3), source, target, f_send.at[s * 6 + 1], rsem,
             jnp.maximum(z - 1, 0), d)
        send(have, source, target, f_send.at[s * 6 + 2], rsem, z, across)
        send(have, source, target, f_send.at[s * 6 + 3], rsem, z, sib)

    order = (z, z + 1 - 2 * slot, jnp.where(z < 2, 2, 1), jnp.where(z < 2, 3, 0))
    local(z <= d, f_ref, fall.at[z, d], f_recv.at[z * 4 + d])
    fan(0, z, f_ref)

    def start_inputs(part):
        cols = pl.ds(part * hw, hw)
        needed = (z >= 2) if part else (z >= 0)
        spot = pl.ds(pl.multiple_of(slot * tb, tb), tb)
        for i in range(2):
            kid = 2 * h + i
            n = part * 2 + i
            for narrow in (True, False):
                width = hw // 2 if narrow else hw
                chosen = needed & ((z == 2 * part) if narrow else (z != 2 * part))
                source = kid_ref.at[i, :, pl.ds(part * hw, width)]
                target = kidf.at[part, z, :, pl.ds(0, width)]
                send((kid != z) & chosen, source, target, kid_send.at[n], kid_recv.at[part * 4 + z], kid, d)
                local((kid == z) & chosen, source, target, kid_recv.at[part * 4 + z])
            send(kid != z, off_ref.at[i, :, cols], offb.at[part, spot, :],
                 off_send.at[n], off_recv.at[part * 2 + slot], kid, home)
            local(kid == z, off_ref.at[i, :, cols], offb.at[part, spot, :], off_recv.at[part * 2 + slot])

    start_inputs(1)
    send(is_keeper, keep_ref.at[slot], kept, k_send.at[0], k_recv.at[0], z, sib)
    local(is_keeper, keep_ref.at[slot], kept, k_recv.at[0])

    def pass_on(s):
        r = order[s]
        _, c = columns(r)
        target, rsem = fall.at[r, c], f_recv.at[r * 4 + c]
        arrived(r <= c, target, rsem)
        send(r <= c, target, target, f_send.at[s * 6 + 4], rsem, z, sib)
        send((r <= c) & (r == 3) & (z == 3), target, target, f_send.at[s * 6 + 5], rsem,
             jnp.maximum(z - 1, 0), d)

    for s in range(1, 4):
        if s == 3:
            start_inputs(0)
        pass_on(s - 1)
        r = order[s]
        c, _ = columns(r)
        arrived(r <= c, fall.at[r, c], f_recv.at[r * 4 + c])
        fan(s, r, fall.at[r, c])
    pass_on(3)
    arrived(z >= 0, kept, k_recv.at[0])
    def outer_block(r, c):
        acc[...] = jnp.zeros_like(acc)

        @pl.loop(jnp.maximum(r, c), 4)
        def _(k):
            acc[...] += dot(fall[r, k], fall[c, k], 1)

    half = pl.multiple_of(h * 2 * tb, 2 * tb)
    def make_product(part):
        low = 2 if part else 0
        for zp in range(low, 4):
            view = kid_view(part, zp)
            arrived(z >= 0, view, kid_recv.at[part * 4 + zp])
            send(is_keeper, view, view, kid_fwd.at[part * 4 + zp],
                 kid_recv.at[part * 4 + zp], z, sib)
        for q in range(2):
            arrived(z >= 0, offb.at[part, pl.ds(q * tb, tb), :], off_recv.at[part * 2 + q])

        @pl.loop(0, 2 * tb // 256)
        def _(m):
            rows = pl.ds(pl.multiple_of(m * 256, 256), 256)
            lower = kidf[part, 2:4].reshape(2 * kr, hw)
            total = dot(offb[1, rows, :], lower, 0)
            if part == 0:
                total += dot(offb[0, rows, :], kidf[0, 0:2].reshape(2 * kr, hw), 0)
            for t in range(2):
                cut = total[t * RB:(t + 1) * RB] * kept[h * 8 + m * 2 + t][0:1]
                prod[part, pl.ds(pl.multiple_of(half + m * 256 + t * RB, RB), RB), :] = cut.astype(jnp.bfloat16)

        mine = prod.at[part, pl.ds(half, 2 * tb), :]
        send(z >= 0, mine, mine, p_send.at[part], p_recv.at[part], z, sib)

        vsum[part] = jnp.zeros((8, hw), jnp.float32)

        @pl.when(h == 0)
        def _():
            for zp in range(low, 4):
                square = jnp.square(kidf[part, zp].astype(jnp.float32))
                vsum[part] += jnp.sum(square.reshape(kr // 8, 8, hw), axis=0)

    def make_cross(part):
        cols = pl.ds(part * hw, hw)
        def ship(i):
            there = 2 * h + i
            send(there != z, cbuf.at[part, i], cross_ref.at[slot, :, cols], c_send.at[part * 2 + i],
                 c_recv.at[part * 2 + slot], there, home)
            local(there == z, cbuf.at[part, i], cross_ref.at[slot, :, cols], c_recv.at[part * 2 + slot])

        theirs = prod.at[part, pl.ds(pl.multiple_of((1 - h) * 2 * tb, 2 * tb), 2 * tb), :]
        arrived(z >= 0, theirs, p_recv.at[part])
        for i in range(2):
            for m in range(2):
                rows = pl.ds(m * (tb // 2), tb // 2)
                total = dot(th[i, 0, rows, :], prod[part, 0:tb, :], 0)
                for j in range(1, 4):
                    total += dot(th[i, j, rows, :], prod[part, j * tb:(j + 1) * tb, :], 0)
                own = prod[part, pl.ds(pl.multiple_of(half + i * tb + m * (tb // 2), tb // 2), tb // 2), :]
                vsum[part] += jnp.sum((own.astype(jnp.float32) * total).reshape(tb // 16, 8, hw), axis=0)
                cbuf[part, i, rows, :] = (-total).astype(jnp.bfloat16)
            if part:
                ship(i)
        for there in range(4):
            to_self = (there == z) & is_keeper
            place = part * 4 + slot * 2 + h
            send(jnp.logical_not(to_self), vsum.at[part], vgot.at[place], v_send.at[part * 4 + there],
                 v_recv.at[place], there, home)
            local(to_self, vsum.at[part], vgot.at[place], v_recv.at[place])
        if not part:
            ship(0)
            ship(1)

    make_product(1)
    arrived(z <= d, fall.at[z, d], f_recv.at[z * 4 + d])
    for s in range(4):
        for c in (sib, far):
            arrived(order[s] <= c, fall.at[order[s], c], f_recv.at[order[s] * 4 + c])

    @pl.loop(0, 8)
    def _(n):
        i, j = lax.div(n, 4), lax.rem(n, 4)
        outer_block(2 * h + i, j)
        th[i, j] = acc[...].astype(jnp.bfloat16)

    make_cross(1)
    make_product(0)
    make_cross(0)
    outer_block(z, d)
    cov_ref[...] = acc[...]

    for part in (1, 0):
        cols = pl.ds(part * hw, hw)
        for q in range(2):
            for hh in range(2):
                arrived(z >= 0, vgot.at[part * 4 + q * 2 + hh], v_recv.at[part * 4 + q * 2 + hh])
            both = vgot[part * 4 + q * 2] + vgot[part * 4 + q * 2 + 1]
            var_ref[q:q + 1, cols] = jnp.sum(both, axis=0, keepdims=True)
    groups = lax.broadcasted_iota(jnp.int32, (G, 2 * hw), 0)
    sums = jnp.zeros((G, 128), jnp.float32)
    counts = jnp.zeros((G, 128), jnp.float32)
    for q in range(2):
        hit = groups == lab_ref[q:q + 1, :]
        terms = jnp.where(hit, var_ref[q:q + 1, :], 0.0)
        ones = jnp.where(hit, 1.0, 0.0)
        for t in range(2 * hw // 128):
            sums += terms[:, t * 128:(t + 1) * 128]
            counts += ones[:, t * 128:(t + 1) * 128]
    tally[d, 0] = sums
    tally[d, 1] = counts
    for n, c in enumerate((sib, across, far)):
        send(z >= 0, tally.at[d], tally.at[d], t_send.at[n], t_recv.at[d], z, c)
    for c in (sib, across, far):
        arrived(z >= 0, tally.at[c], t_recv.at[c])
    sums = tally[0, 0] + tally[1, 0] + tally[2, 0] + tally[3, 0]
    counts = tally[0, 1] + tally[1, 1] + tally[2, 1] + tally[3, 1]
    mean = jnp.sum(sums, axis=1, keepdims=True) / jnp.sum(counts, axis=1, keepdims=True)
    mean_ref[...] = jnp.broadcast_to(mean, mean_ref.shape)
    for part in (1, 0):
        for q in range(2):
            place = cross_ref.at[q, :, pl.ds(part * hw, hw)]
            arrived(z >= 0, place, c_recv.at[part * 2 + q])
    for cond, copy in pending:
        pl.when(cond)(copy.wait_send)


def per_device_fused(top_inv, off_block, kid_inv, row_struct, labels):
    row_rank = lax.axis_index("srow")
    col_rank = lax.axis_index("scol")
    tb = top_inv.shape[0]
    row_ids = row_rank * tb + jnp.arange(tb, dtype=jnp.int32)
    col_ids = col_rank * tb + jnp.arange(tb, dtype=jnp.int32)
    diagonal_one = (col_ids[None, :] == row_ids[:, None]).astype(top_inv.dtype)
    top_factor = jnp.where(col_ids[None, :] > row_ids[:, None], top_inv, diagonal_one)
    kr = kid_inv.shape[1]
    width = kid_inv.shape[2]
    hw = width // 2
    kid_row_ids = row_rank * kr + jnp.arange(kr, dtype=jnp.int32)
    kid_col_ids = jnp.arange(width, dtype=jnp.int32)
    kid_one = (kid_row_ids[:, None] == kid_col_ids[None, :]).astype(kid_inv.dtype)
    kid_factor = jnp.where(kid_row_ids[:, None] > kid_col_ids[None, :], kid_inv, kid_one)
    keep = jnp.broadcast_to(
        (row_struct != 0).astype(jnp.float32)[:, :, None, None], row_struct.shape + (8, hw)
    )
    bf = jnp.bfloat16
    dma = pltpu.SemaphoreType.DMA
    top_cov, cross_half, node_var, means = pl.pallas_call(
        fused,
        out_shape=(
            jax.ShapeDtypeStruct((tb, tb), jnp.float32),
            jax.ShapeDtypeStruct((2, tb, width), bf),
            jax.ShapeDtypeStruct((2, width), jnp.float32),
            jax.ShapeDtypeStruct((G, 128), jnp.float32),
        ),
        in_specs=[pl.BlockSpec(memory_space=pl.ANY)] * 4 + [pl.BlockSpec(memory_space=pltpu.VMEM)],
        out_specs=(
            pl.BlockSpec(memory_space=pltpu.VMEM),
            pl.BlockSpec(memory_space=pl.ANY),
            pl.BlockSpec(memory_space=pltpu.VMEM),
            pl.BlockSpec(memory_space=pltpu.VMEM),
        ),
        scratch_shapes=[
            pltpu.VMEM((4, 4, tb, tb), bf),
            pltpu.VMEM((2, 2 * tb, hw), bf),
            pltpu.VMEM((2, 4, kr, hw), bf),
            pltpu.VMEM((2, 4 * tb, hw), bf),
            pltpu.VMEM((2, 4, tb, tb), bf),
            pltpu.VMEM((tb, tb), jnp.float32),
            pltpu.VMEM((2, 2, tb, hw), bf),
            pltpu.VMEM((2, 8, hw), jnp.float32),
            pltpu.VMEM((8, 8, hw), jnp.float32),
            pltpu.VMEM((row_struct.shape[1], 8, hw), jnp.float32),
            pltpu.VMEM((4, 2, G, 128), jnp.float32),
            dma((24,)), dma((16,)), dma((4,)), dma((4,)), dma((4,)), dma((8,)), dma((8,)),
            dma((2,)), dma((2,)), dma((4,)), dma((4,)), dma((8,)), dma((8,)),
            dma((1,)), dma((1,)), dma((3,)), dma((4,)),
        ],
        compiler_params=pltpu.CompilerParams(
            collective_id=0, has_side_effects=True, vmem_limit_bytes=48 * 1024 * 1024
        ),
    )(top_factor, off_block, kid_factor, keep, labels)
    return (top_cov, cross_half.astype(jnp.float32), node_var, means[:, 0])


def solution(mesh):
    placed = (
        P(("basin", "srow"), "scol"),
        P(("basin", "scol"), "srow", None),
        P(("basin", "scol"), "srow", None),
        P(("basin", "scol"), None),
        P(("basin", "scol"), None),
    )
    small = mesh.shape["srow"] == 4 and mesh.shape["scol"] == 4
    return jax.shard_map(
        per_device_fused if small else per_device,
        mesh=mesh,
        in_specs=placed,
        out_specs=(
            P(("basin", "srow"), "scol"),
            P(("basin", "scol"), "srow", None),
            P(("basin", "scol"), None),
            P("basin"),
        ),
        check_vma=False,
    )
```
